256 devices in a mesh: rows: 64 (over z, y, core), section: 4 (over x).
Axes of the slice: x: 4, y: 4, z: 8, core: 2. Of those that a mesh axis runs over, the one named last changes fastest.
Arguments:
- block_out: bfloat16 [4, 64, 128, 512], P('section', 'rows'), may hold values from -6 to 6
- out_grad: bfloat16 [4, 64, 128, 512], P('section', 'rows'), may hold values from -6 to 6
- weights: bfloat16 [4, 2, 2304, 256], P('section'), may hold values from -0.125 to 0.125
Outputs:
- restored: bfloat16 [4, 64, 128, 512], P('section', 'rows')
- input_grad: bfloat16 [4, 64, 128, 512], P('section', 'rows')
- weight_grad: float32 [4, 2, 2304, 256], P('section', None, 'rows')
The draws below stay inside these ranges and needn't reach their ends.
All inputs are finite; a program needn't handle non-finite values.
Results may differ from the reference program's by a relative error of at most 0.025.
Values may be sent and summed in bfloat16 or wider, within the bound.
No kernel may reach another device: no remote copies, remote signals or barrier semaphores. Data moves between devices by JAX's collectives and lax.ppermute only.
A program may use at most 128 MiB of HBM per device.

```python
import math
import jax
import jax.numpy as jnp
from jax import lax

HALF = 256
WIDTH = 512
COLS = 128
ROWS = 64
MICRO = 4
BLOCKS = 4


def level_of(own_key, extent, cuts, least, largest):
    level = 1.0
    for axis_at, parts in cuts:
        draws = jax.random.uniform(jax.random.fold_in(jax.random.fold_in(own_key, 6), axis_at), (parts,), jnp.float32, least / len(cuts), largest / len(cuts))
        level = level * jnp.repeat(jnp.exp(draws), extent[axis_at] // parts).reshape((-1,) + (1,) * (len(extent) - 1 - axis_at))
    return level


def gaussian(key, dims, scale, reach, cuts=(), kind=jnp.bfloat16):
    result = jax.random.normal(key, dims, jnp.float32) * scale
    if len(cuts) > 0:
        result = level_of(key, dims, cuts, -0.22, 0.18) * result
    return jnp.clip(result, min=-reach, max=reach).astype(kind)


def setup_inputs(seed: int = 0) -> dict:
    arg_keys = jax.random.split(jax.random.key(seed), 4)
    return {
        "block_out": gaussian(arg_keys[0], (MICRO, ROWS, COLS, WIDTH), 1.0, 6.0, ((0, 4), (1, 64))),
        "out_grad": gaussian(arg_keys[1], (MICRO, ROWS, COLS, WIDTH), 1.0, 6.0, ((0, 4), (1, 64))),
        "weights": gaussian(arg_keys[2], (BLOCKS, 2, 9 * HALF, HALF), (9 * HALF) ** -0.5, 0.125, ((0, 4),)),
    }


def column_pad(field):
    return jnp.pad(field, ((0, 0), (1, 1), (0, 0)))

def row_pad(field):
    return jnp.pad(field, ((1, 1), (0, 0), (0, 0)))

def stencil_taps(padded, height, across, flipped):
    pieces = []
    for row_off in range(3):
        for col_off in range(3):
            row_start = 2 - row_off if flipped else row_off
            col_start = 2 - col_off if flipped else col_off
            pieces.append(padded[row_start:row_start + height, col_start:col_start + across])
    return jnp.concatenate(pieces, axis=-1).reshape(height * across, -1)

def turned_weight(weight):
    channels = weight.shape[1]
    return weight.reshape(9, channels, channels).transpose(0, 2, 1).reshape(9 * channels, channels)

def silu_slope(pre_value, sig_value):
    return sig_value * (1.0 + pre_value * (1.0 - sig_value))

def block_backward(field, cotangent, weight_f, weight_g, extend):
    height, across, width = field.shape
    half = width // 2
    first = field[..., :half]
    second = field[..., half:]
    grad_first = cotangent[..., :half].reshape(-1, half).astype(jnp.float32)
    grad_second = cotangent[..., half:].reshape(-1, half).astype(jnp.float32)
    taps_first = stencil_taps(column_pad(extend(first)), height, across, False)
    pre_g = jnp.dot(taps_first, weight_g, preferred_element_type=jnp.float32)
    sig_g = jax.nn.sigmoid(pre_g)
    input_second = (second.reshape(-1, half).astype(jnp.float32) - pre_g * sig_g).astype(jnp.bfloat16)
    taps_second = stencil_taps(column_pad(extend(input_second.reshape(height, across, half))), height, across, False)
    pre_f = jnp.dot(taps_second, weight_f, preferred_element_type=jnp.float32)
    sig_f = jax.nn.sigmoid(pre_f)
    input_first = (first.reshape(-1, half).astype(jnp.float32) - pre_f * sig_f).astype(jnp.bfloat16)
    delta_g = (grad_second * silu_slope(pre_g, sig_g)).astype(jnp.bfloat16)
    grad_wg = lax.dot_general(taps_first, delta_g, (((0,), (0,)), ((), ())), preferred_element_type=jnp.float32)
    taps_back_g = stencil_taps(column_pad(extend(delta_g.reshape(height, across, half))), height, across, True)
    back_g = jnp.dot(taps_back_g, turned_weight(weight_g), preferred_element_type=jnp.float32)
    total_first = (grad_first + back_g).astype(jnp.bfloat16)
    delta_f = (total_first.astype(jnp.float32) * silu_slope(pre_f, sig_f)).astype(jnp.bfloat16)
    grad_wf = lax.dot_general(taps_second, delta_f, (((0,), (0,)), ((), ())), preferred_element_type=jnp.float32)
    taps_back_f = stencil_taps(column_pad(extend(delta_f.reshape(height, across, half))), height, across, True)
    back_f = jnp.dot(taps_back_f, turned_weight(weight_f), preferred_element_type=jnp.float32)
    total_second = (grad_second + back_f).astype(jnp.bfloat16)
    restored = jnp.concatenate([input_first, input_second], axis=-1).reshape(height, across, width)
    grads_in = jnp.concatenate([total_first, total_second], axis=-1).reshape(height, across, width)
    return (restored, grads_in, grad_wf, grad_wg)

def reference(block_out, out_grad, weights):
    micro_count = block_out.shape[0]
    block_count = weights.shape[0]
    scale = 1.0 / math.sqrt(MICRO * ROWS * COLS)
    grad_sum = jnp.zeros(weights.shape, jnp.float32)
    restored_all = []
    grads_all = []
    for micro in range(micro_count):
        field = block_out[micro]
        cotangent = out_grad[micro]
        for block in reversed(range(block_count)):
            field, cotangent, grad_wf, grad_wg = block_backward(field, cotangent, weights[block, 0], weights[block, 1], row_pad)
            grad_sum = grad_sum.at[block].add(jnp.stack([grad_wf, grad_wg]))
        restored_all.append(field)
        grads_all.append(cotangent)
    return (jnp.stack(restored_all), jnp.stack(grads_all), grad_sum * scale)
```

```python
import functools
import math

import jax
import jax.numpy as jnp
from jax import lax
from jax.experimental import pallas as pl
from jax.experimental.pallas import tpu as pltpu
from jax.sharding import PartitionSpec as P

HALF=256; TR=8; TC=16

def row_chunks(rows, most):
    n = -(-rows // most)
    base, extra = divmod(rows, n)
    out=[]; a=0
    for i in range(n):
        b = base + (1 if i < extra else 0)
        out.append((a, b)); a += b
    return out

def block_kernel(p, W, WN, most, meta, y1, y2, g1, g2, wa, wb, x1o, x2o, t1o, n2o, ay, ax, dgo, dfo, w, s1, s2, s3, s4, sems):
    C = HALF
    core, rowbase, colbase = meta[0], meta[1], meta[2]
    ca = pltpu.make_async_copy(wa, w.at[core], sems.at[0])
    cb = pltpu.make_async_copy(wb, w.at[1 - core], sems.at[1])
    ca.start(); cb.start()
    first = 8 + 2 * (p + 1)
    own = (W - TC) // 2
    cut = (W - WN) // 2

    def spread(buf, at, value):
        n = value.shape[0]
        flat = value.reshape(n * W, C)
        buf[at * W:(at + n) * W, 0:C] = pltpu.roll(flat, 1, 0).astype(jnp.bfloat16)
        buf[at * W:(at + n) * W, C:2 * C] = flat.astype(jnp.bfloat16)
        buf[at * W:(at + n) * W, 2 * C:3 * C] = pltpu.roll(flat, n * W - 1, 0).astype(jnp.bfloat16)

    def mask(a, n, halo):
        r = lax.broadcasted_iota(jnp.int32, (n, W, 1), 0) + (rowbase - halo + a)
        c = lax.broadcasted_iota(jnp.int32, (n, W, 1), 1) + (colbase - own)
        return (r >= 0) & (r < 64) & (c >= 0) & (c < 128)

    def conv(buf, a, n, branch):
        acc = None
        for dr in range(3):
            d = jnp.dot(buf[(a + dr) * W:(a + dr + n) * W, :], w[branch, 768 * dr:768 * (dr + 1), :],
                        preferred_element_type=jnp.float32)
            acc = d if acc is None else acc + d
        return acc.reshape(n, W, C)

    def conv_t(buf, a, n, branch):
        acc = None
        for dr in range(3):
            for dc in range(3):
                tap = 3 * dr + dc
                d = lax.dot_general(buf[(a + 2 - dr) * W:(a + 2 - dr + n) * W, (2 - dc) * C:(3 - dc) * C],
                                    w[branch, 256 * tap:256 * (tap + 1), :],
                                    (((1,), (1,)), ((), ())), preferred_element_type=jnp.float32)
                acc = d if acc is None else acc + d
        return acc.reshape(n, W, C)

    for a, n in row_chunks(first, most):
        spread(s1, a, y1[a:a + n].astype(jnp.float32))
    ca.wait(); cb.wait()
    for a, n in row_chunks(8 + 2 * p, most):
        pre = conv(s1, a, n, 1)
        sig = jax.nn.sigmoid(pre)
        x2 = jnp.where(mask(a, n, p), y2[a:a + n].astype(jnp.float32) - pre * sig, 0.0)
        x2 = x2.astype(jnp.bfloat16).astype(jnp.float32)
        spread(s2, a, x2)
        dg = g2[a:a + n].astype(jnp.float32) * (sig * (1.0 + pre * (1.0 - sig)))
        spread(s3, a, dg.astype(jnp.bfloat16).astype(jnp.float32))
    for a, n in row_chunks(8 + 2 * (p - 1), most):
        pre = conv(s2, a, n, 0)
        sig = jax.nn.sigmoid(pre)
        m = mask(a, n, p - 1)
        x1 = jnp.where(m, y1[a + 2:a + 2 + n].astype(jnp.float32) - pre * sig, 0.0)
        t1 = jnp.where(m, g1[a:a + n].astype(jnp.float32) + conv_t(s3, a, n, 1), 0.0)
        t1 = t1.astype(jnp.bfloat16).astype(jnp.float32)
        df = t1 * (sig * (1.0 + pre * (1.0 - sig)))
        spread(s4, a, df.astype(jnp.bfloat16).astype(jnp.float32))
        store(x1o, x1, a, n, p - 1, cut, WN)
        store(t1o, t1, a, n, p - 1, cut, WN)
    for a, n in row_chunks(8 + 2 * (p - 2), most):
        n2 = jnp.where(mask(a, n, p - 2), g2[a + 2:a + 2 + n].astype(jnp.float32) + conv_t(s4, a, n, 0), 0.0)
        store(n2o, n2, a, n, p - 2, cut, WN)
    rows2 = x2o.shape[0]; off = (8 + 2 * p - rows2) // 2
    x2 = s2[off * W:(off + rows2) * W, C:2 * C].astype(jnp.float32).reshape(rows2, W, C)
    x2o[...] = x2[:, cut:cut + WN].astype(jnp.bfloat16)
    e = own - 8
    for dst, src, h in ((ay, s1, p + 1), (ax, s2, p)):
        v = src[(h - 1) * W:(h + 9) * W, C:2 * C].astype(jnp.float32).reshape(10, W, C)
        dst[...] = v[:, e:e + 32].astype(jnp.bfloat16)
    for dst, src, h in ((dgo, s3, p), (dfo, s4, p - 1)):
        v = src[h * W:(h + 8) * W, C:2 * C].astype(jnp.float32).reshape(8, W, C)
        dst[...] = v[:, own:own + TC].astype(jnp.bfloat16)

def store(ref, value, a, n, halo, cut, WN):
    rows = ref.shape[0]; off = (8 + 2 * halo - rows) // 2
    lo, hi = max(a, off), min(a + n, off + rows)
    if lo < hi:
        ref[lo - off:hi - off] = value[lo - a:hi - a, cut:cut + WN].astype(jnp.bfloat16)

def block(p, W, WN, meta, y1, y2, g1, g2, wa, wb, most=8):
    C = HALF; b = jnp.bfloat16
    q = max(p - 2, 0)
    rows_x1 = 8 + 2 * (p - 1) if p > 2 else 8
    outs = [(rows_x1, WN), (8 + 2 * q, WN), (8 + 2 * max(p - 3, 0), WN), (8 + 2 * q, WN), (10, 32), (10, 32), (8, TC), (8, TC)]
    V = pl.BlockSpec(memory_space=pltpu.VMEM)
    flops = 2 * 2304 * 256 * W * 2 * (4 * (8 + 2 * p) - 8)
    return pl.pallas_call(
        functools.partial(block_kernel, p, W, WN, most),
        out_shape=[jax.ShapeDtypeStruct((r, w_, C), b) for r, w_ in outs],
        in_specs=[pl.BlockSpec(memory_space=pltpu.SMEM), V, V, V, V, pl.BlockSpec(memory_space=pl.ANY), pl.BlockSpec(memory_space=pl.ANY)],
        out_specs=[V] * 8,
        scratch_shapes=[pltpu.VMEM((2, 2304, C), b)] + [pltpu.VMEM(((8 + 2 * (p + 1 - i)) * W, 3 * C), b) for i in (0, 1, 1, 2)] + [pltpu.SemaphoreType.DMA((2,))],
        compiler_params=pltpu.CompilerParams(vmem_limit_bytes=40 * 1024 * 1024),
        cost_estimate=pl.CostEstimate(flops=flops, bytes_accessed=6 * 1024 * 1024, transcendentals=0),
        name="block_p%d" % p,
    )(meta, y1, y2, g1, g2, wa, wb)


def grad_kernel(meta, acts, send, mine, lhs):
    C = HALF
    core = meta[0]
    for branch, out in ((1 - core, send), (core, mine)):
        for m in range(4):
            v = acts[m, branch, 0:320, :].astype(jnp.float32)
            for dc, shifted in enumerate((pltpu.roll(v, 1, 0), v, pltpu.roll(v, 319, 0))):
                s = shifted.reshape(10, 32, C)[:, 8:24].astype(jnp.bfloat16)
                for dr in range(3):
                    t = 3 * dr + dc
                    lhs[m * 128:(m + 1) * 128, t * C:(t + 1) * C] = s[dr:dr + 8].reshape(128, C)
        d = jnp.concatenate([acts[m, branch, 320:448, :] for m in range(4)], axis=0)
        for t in range(9):
            g = lax.dot_general(lhs[:, t * C:(t + 1) * C], d, (((0,), (0,)), ((), ())),
                                preferred_element_type=jnp.float32)
            out[t * C:(t + 1) * C, :] = g.astype(out.dtype)


def kernel_grads(meta, acts):
    V = pl.BlockSpec(memory_space=pltpu.VMEM)
    return pl.pallas_call(
        grad_kernel,
        out_shape=[jax.ShapeDtypeStruct((2304, HALF), jnp.bfloat16), jax.ShapeDtypeStruct((2304, HALF), jnp.float32)],
        in_specs=[pl.BlockSpec(memory_space=pltpu.SMEM), V],
        out_specs=[V, V],
        scratch_shapes=[pltpu.VMEM((512, 2304), jnp.bfloat16)],
        compiler_params=pltpu.CompilerParams(vmem_limit_bytes=40 * 1024 * 1024),
        cost_estimate=pl.CostEstimate(flops=4 * 512 * 2304 * 256, bytes_accessed=8 * 1024 * 1024, transcendentals=0),
        name="kernel_grads",
    )(meta, acts)


def device(z, y, c):
    return (z * 4 + y) * 2 + c


PLANE = [[device(z, y, c) for y in range(4) for c in range(2)] for z in range(8)]
YLINE = [[device(z, y, c) for y in range(4)] for z in range(8) for c in range(2)]
ZLINE = [[device(z, y, c) for z in range(8)] for y in range(4) for c in range(2)]
CORES = [(i, i ^ 1) for i in range(64)]


def along_z(value, by):
    pairs = [(i, i + 8 * by) for i in range(64) if 0 <= i + 8 * by < 64]
    return lax.ppermute(value, "rows", pairs)


def exchange(value, groups):
    return lax.all_to_all(value, "rows", 0, 0, axis_index_groups=groups)


def local(block_out, out_grad, weights):
    C = HALF
    place = lax.axis_index("rows")
    z, j = place // 8, place % 8
    y, core = j // 2, place % 2
    meta = jnp.stack([core, 8 * z, 16 * j]).astype(jnp.int32)

    own = weights[0].reshape(4608, C)
    part = lax.dynamic_slice_in_dim(own, core * 2304 + y * 576, 576, 0)
    parts = lax.all_to_all(jnp.broadcast_to(part[None], (4, 576, C)), "section", 0, 0)

    pair = jnp.concatenate([block_out[0, 0], out_grad[0, 0]], axis=-1)
    padded = jnp.pad(pair, ((16, 16), (0, 0)))
    pieces = jnp.stack([padded[16 * i + 4:16 * i + 44] for i in range(8)])
    tile = exchange(pieces, PLANE)
    above = along_z(tile, 1)
    below = along_z(tile, -1)
    far_above = along_z(tile[7, :, :C], 2)
    far_below = along_z(tile[0, :, :C], -2)
    wide = lambda v: jnp.pad(v, ((0, 0), (4, 4), (0, 0)))
    y1 = wide(jnp.concatenate([far_above[None], above[..., :C], tile[..., :C], below[..., :C], far_below[None]], axis=0))
    y2, g1, g2 = (wide(jnp.concatenate([above[..., i * C:(i + 1) * C], tile[..., i * C:(i + 1) * C], below[..., i * C:(i + 1) * C]], axis=0)) for i in (1, 2, 3))
    g1 = g1[1:-1]

    acts = [None] * 4
    for k, p, W, WN in ((3, 8, 48, 32), (2, 6, 32, 32), (1, 4, 32, 32), (0, 2, 32, 16)):
        mine = exchange(jnp.broadcast_to(parts[k][None], (4, 576, C)), YLINE).reshape(2304, C)
        other = lax.ppermute(mine, "rows", CORES)
        y1, y2, g1, g2, ay, ax, dg, df = block(p, W, WN, meta, y1, y2, g1, g2, mine, other)
        acts[k] = jnp.concatenate([v.reshape(-1, C) for v in (ax, df, ay, dg)], axis=0)

    done = exchange(jnp.concatenate([y1, y2, g1, g2], axis=-1), PLANE).reshape(128, 4 * C)
    restored = done[:, :2 * C][None, None]
    input_grad = done[:, 2 * C:][None, None]

    gathered = lax.all_to_all(jnp.stack(acts), "section", 0, 0).reshape(4, 2, 448, C)
    away, kept = kernel_grads(meta, gathered)
    kept = kept + lax.ppermute(away, "rows", CORES).astype(jnp.float32)
    kept = kept.astype(jnp.bfloat16).reshape(8, 4, 72, C).transpose(1, 0, 2, 3).reshape(4, 576, C)
    kept = jnp.sum(exchange(kept, YLINE).astype(jnp.float32), axis=0)
    kept = kept.astype(jnp.bfloat16).reshape(8, 72, C)
    kept = jnp.sum(exchange(kept, ZLINE).astype(jnp.float32), axis=0)
    here = lax.dynamic_slice_in_dim(kept, 36 * core, 36, 0)
    there = lax.ppermute(lax.dynamic_slice_in_dim(kept, 36 * (1 - core), 36, 0), "rows", CORES)
    grad = jnp.where(core == 0, jnp.stack([here, there]), jnp.stack([there, here]))
    return restored, input_grad, (grad * (1.0 / math.sqrt(32768)))[None]


def solution(mesh):
    spec = P("section", "rows", None, None)
    return jax.shard_map(
        local,
        mesh=mesh,
        in_specs=(spec, spec, P("section", None, None, None)),
        out_specs=(spec, spec, P("section", None, "rows", None)),
        check_vma=False,
    )
```

```python
import math

import jax
import jax.numpy as jnp
from jax import lax
from jax.experimental import pallas as pl
from jax.experimental.pallas import tpu as pltpu
from jax.sharding import Mesh
from jax.sharding import PartitionSpec as P

C = 256
W = 32
WIDE = 48
PIECE = WIDE + 3 * W
QUARTER = 576
SPAN = 18
VMEM = pl.BlockSpec(memory_space=pltpu.VMEM)
SMEM = pl.BlockSpec(memory_space=pltpu.SMEM)
HBM = pl.BlockSpec(memory_space=pltpu.HBM)
PARAMS = pltpu.CompilerParams(vmem_limit_bytes=24 * 1024 * 1024)
f32, bf16 = jnp.float32, jnp.bfloat16


def row_chunks(rows, most=8):
    count = -(-rows // most)
    base, extra = divmod(rows, count)
    out, at = [], 0
    for i in range(count):
        size = base + (1 if i < extra else 0)
        out.append((at, size))
        at += size
    return out


def pieces_kernel(field, cotangent, out, padded):
    padded[0:16] = jnp.zeros((16, 4 * C), f32)
    padded[144:160] = jnp.zeros((16, 4 * C), f32)
    padded[16:144, 0:2 * C] = field[...].astype(f32)
    padded[16:144, 2 * C:4 * C] = cotangent[...].astype(f32)
    for j in range(8):
        out[j, 0:WIDE] = padded[16 * j:16 * j + WIDE, 0:C].astype(bf16)
        for i in range(1, 4):
            at = WIDE + (i - 1) * W
            out[j, at:at + W] = padded[16 * j + 8:16 * j + 8 + W, i * C:(i + 1) * C].astype(bf16)


def make_pieces(field, cotangent):
    return pl.pallas_call(
        pieces_kernel,
        out_shape=jax.ShapeDtypeStruct((8, PIECE, C), bf16),
        in_specs=[VMEM, VMEM],
        out_specs=VMEM,
        scratch_shapes=[pltpu.VMEM((160, 4 * C), f32)],
        compiler_params=PARAMS,
        name="pieces",
    )(field, cotangent)


def blocks_kernel(meta, above, tile, below, far_above, far_below, held, one, one2, three, three2, *refs):
    quarters, (done, acts, w, s1a, s1b, s2a, s2b, s3, s4, t1a, t1b, n2a, n2b, packed, sent, sems) = refs[:8], refs[8:]
    core, rowbase, place, section, y = (meta[i] for i in range(5))
    colbase = 16 * place

    def kernel_copy(k, branch, src, at=0):
        size = src.shape[0]
        return pltpu.make_async_copy(src, w.at[k, branch, pl.ds(at, size)], sems.at[2 * k + jnp.where(branch == core, 0, 1)])

    for k in (3, 2, 1, 0):
        ahead = lax.rem(k + 4 - section, 4)

        @pl.when(ahead == 0)
        def _():
            kernel_copy(k, core, held.at[core]).start()
            kernel_copy(k, 1 - core, held.at[1 - core]).start()

        @pl.when(ahead == 1)
        def _():
            kernel_copy(k, core, one).start()
            kernel_copy(k, 1 - core, one2).start()

        @pl.when(ahead == 3)
        def _():
            kernel_copy(k, core, three).start()
            kernel_copy(k, 1 - core, three2).start()

        @pl.when(ahead == 2)
        def _():
            for d in range(4):
                at = pl.multiple_of(lax.rem(y + 4 - d, 4) * QUARTER, QUARTER)
                kernel_copy(k, core, quarters[d], at).start()
                kernel_copy(k, 1 - core, quarters[4 + d], at).start()

    def put(buf, at, mid, left, right):
        n = mid.shape[0]
        rows = slice(at * W, (at + n) * W)
        buf[rows, 0:C] = left.reshape(n * W, C).astype(bf16)
        buf[rows, C:2 * C] = mid.reshape(n * W, C).astype(bf16)
        buf[rows, 2 * C:3 * C] = right.reshape(n * W, C).astype(bf16)

    def spread(buf, at, value):
        n, wide = value.shape[0], value.shape[1]
        flat = value.reshape(n * wide, C)
        left = pltpu.roll(flat, 1, 0).reshape(n, wide, C)
        right = pltpu.roll(flat, n * wide - 1, 0).reshape(n, wide, C)
        cut = (wide - W) // 2
        put(buf, at, *(v[:, cut:cut + W] for v in (value, left, right)))

    def inside(a, n, halo):
        r = lax.broadcasted_iota(jnp.int32, (n, W, 1), 0) + (rowbase - halo + a)
        c = lax.broadcasted_iota(jnp.int32, (n, W, 1), 1) + (colbase - 8)
        return (r >= 0) & (r < 64) & (c >= 0) & (c < 128)

    def conv(buf, a, n, k, branch):
        acc = None
        for dr in range(3):
            d = jnp.dot(buf[(a + dr) * W:(a + dr + n) * W, :], w[k, branch, 768 * dr:768 * (dr + 1), :],
                        preferred_element_type=f32)
            acc = d if acc is None else acc + d
        return acc.reshape(n, W, C)

    def conv_t(buf, a, n, k, branch):
        acc = None
        for dr in range(3):
            for dc in range(3):
                tap = 3 * dr + dc
                d = lax.dot_general(buf[(a + 2 - dr) * W:(a + 2 - dr + n) * W, (2 - dc) * C:(3 - dc) * C],
                                    w[k, branch, 256 * tap:256 * (tap + 1), :],
                                    (((1,), (1,)), ((), ())), preferred_element_type=f32)
                acc = d if acc is None else acc + d
        return acc.reshape(n, W, C)

    def window(lo, hi, a, n, halo):
        parts, at = [], a - halo
        while at < a - halo + n:
            if at < -8:
                part, took = far_above[lo:hi][None], 1
            elif at >= 16:
                part, took = far_below[lo:hi][None], 1
            else:
                ref, base = ((above, -8), (tile, 0), (below, 8))[0 if at < 0 else 1 if at < 8 else 2]
                took = min(a - halo + n, base + 8) - at
                part = ref[at - base:at - base + took, lo:hi]
            parts.append(part.astype(f32))
            at += took
        return parts[0] if len(parts) == 1 else jnp.concatenate(parts, axis=0)

    def lanes(buf, a, n):
        return buf[a * W:(a + n) * W, C:2 * C].astype(f32).reshape(n, W, C)

    def finish(which, value, a, n, halo):
        lo, hi = max(a, halo), min(a + n, halo + 8)
        for i in range(lo, hi):
            at = lax.rem(i - halo + 8 - place, 8)
            done[at, :, which * C:(which + 1) * C] = value[i - a, 8:24].astype(bf16)

    for a, n in row_chunks(26):
        spread(s1a, a, window(0, WIDE, a, n, 9))
    for k, p in ((3, 8), (2, 6), (1, 4), (0, 2)):
        first, last = k == 3, k == 0
        s1, s1n = (s1a, s1b) if k % 2 else (s1b, s1a)
        s2, s2o = (s2a, s2b) if k % 2 else (s2b, s2a)
        t1n, t1o = (t1a, t1b) if k % 2 else (t1b, t1a)
        n2n, n2o = (n2a, n2b) if k % 2 else (n2b, n2a)

        def old_y2(a, n):
            return window(WIDE, WIDE + W, a, n, p) if first else lanes(s2o, a + 2, n)

        def old_g1(a, n):
            return window(WIDE + W, WIDE + 2 * W, a, n, p - 1) if first else t1o[a + 2:a + 2 + n].astype(f32)

        def old_g2(a, n):
            return window(WIDE + 2 * W, WIDE + 3 * W, a, n, p) if first else n2o[a:a + n].astype(f32)

        kernel_copy(k, core, held.at[0]).wait()
        kernel_copy(k, 1 - core, held.at[0]).wait()
        for a, n in row_chunks(8 + 2 * p):
            pre = conv(s1, a, n, k, 1)
            sig = jax.nn.sigmoid(pre)
            x2 = jnp.where(inside(a, n, p), old_y2(a, n) - pre * sig, 0.0)
            x2 = x2.astype(bf16).astype(f32)
            spread(s2, a, x2)
            if last:
                finish(1, x2, a, n, p)
            dg = old_g2(a, n) * (sig * (1.0 + pre * (1.0 - sig)))
            spread(s3, a, dg.astype(bf16).astype(f32))
        for a, n in row_chunks(6 + 2 * p):
            pre = conv(s2, a, n, k, 0)
            sig = jax.nn.sigmoid(pre)
            m = inside(a, n, p - 1)
            x1 = jnp.where(m, lanes(s1, a + 2, n) - pre * sig, 0.0)
            t1 = jnp.where(m, old_g1(a, n) + conv_t(s3, a, n, k, 1), 0.0)
            t1 = t1.astype(bf16).astype(f32)
            df = t1 * (sig * (1.0 + pre * (1.0 - sig)))
            spread(s4, a, df.astype(bf16).astype(f32))
            if last:
                finish(0, x1, a, n, p - 1)
                finish(2, t1, a, n, p - 1)
            else:
                spread(s1n, a, x1.astype(bf16).astype(f32))
                t1n[a:a + n] = t1.astype(bf16)
        for a, n in row_chunks(4 + 2 * p):
            n2 = jnp.where(inside(a, n, p - 2), old_g2(a + 2, n) + conv_t(s4, a, n, k, 0), 0.0)
            if last:
                finish(3, n2, a, n, p - 2)
            else:
                n2n[a:a + n] = n2.astype(bf16)

        for branch, src, h, delta, hd in ((0, s2, p, s4, p - 1), (1, s1, p + 1, s3, p)):
            for i in range(10):
                v = src[(h - 1 + i) * W:(h + i) * W, 0:C].astype(f32)
                packed[SPAN * i:SPAN * i + 24] = v[8:32]
            sent[4 * branch + k, 0:192] = packed[0:192].astype(bf16)
            d = lanes(delta, hd, 8)[:, 8:24]
            sent[4 * branch + k, 192:320] = d.reshape(128, C).astype(bf16)
            pltpu.make_async_copy(sent.at[4 * branch + k], acts.at[4 * branch + k], sems.at[8 + 4 * branch + k]).start()
    for i in range(8):
        pltpu.make_async_copy(sent.at[i], acts.at[i], sems.at[8 + i]).wait()


def blocks(meta, fields, kernels):
    def spread(rows):
        return pltpu.VMEM((rows * W, 3 * C), bf16)

    def plain(rows):
        return pltpu.VMEM((rows, W, C), bf16)

    flops = sum(2 * 2304 * 256 * W * (4 * (8 + 2 * p) - 12) for p in (8, 6, 4, 2))
    return pl.pallas_call(
        blocks_kernel,
        out_shape=[jax.ShapeDtypeStruct((8, 16, 4 * C), bf16), jax.ShapeDtypeStruct((8, 320, C), bf16)],
        in_specs=[SMEM] + [VMEM] * 5 + [HBM] * len(kernels),
        out_specs=[VMEM, HBM],
        scratch_shapes=[pltpu.VMEM((4, 2, 2304, C), bf16), spread(26), spread(22), spread(24), spread(20), spread(24), spread(22),
                        plain(22), plain(18), plain(20), plain(16),
                        pltpu.VMEM((192, C), f32), pltpu.VMEM((8, 320, C), bf16), pltpu.SemaphoreType.DMA((16,))],
        compiler_params=pltpu.CompilerParams(vmem_limit_bytes=56 * 1024 * 1024),
        cost_estimate=pl.CostEstimate(flops=flops, bytes_accessed=16 * 1024 * 1024, transcendentals=0),
        name="blocks",
    )(meta, *fields, *kernels)


def grad_kernel(acts, out, lhs, packed, grad):
    for m in range(8):
        packed[0:192] = acts[m, 0:192].astype(f32)
        for i in range(10):
            for dc in range(3):
                v = packed[SPAN * i + dc:SPAN * i + dc + 16, :].astype(bf16)
                for dr in range(3):
                    if 0 <= i - dr < 8:
                        at, t = m * 128 + (i - dr) * 16, 3 * dr + dc
                        lhs[at:at + 16, t * C:(t + 1) * C] = v
    d = jnp.concatenate([acts[m, 192:320] for m in range(8)], axis=0)
    for t in range(9):
        grad[t * C:(t + 1) * C, :] = lax.dot_general(
            lhs[:, t * C:(t + 1) * C], d, (((0,), (0,)), ((), ())), preferred_element_type=f32)
    for z in range(8):
        for y in range(4):
            at = (4 * z + y) * 72
            out[y, z] = grad[at:at + 72].astype(bf16)


def kernel_grads(acts):
    return pl.pallas_call(
        grad_kernel,
        out_shape=jax.ShapeDtypeStruct((4, 8, 72, C), bf16),
        in_specs=[VMEM],
        out_specs=VMEM,
        scratch_shapes=[pltpu.VMEM((1024, 2304), bf16), pltpu.VMEM((192, C), f32), pltpu.VMEM((2304, C), f32)],
        compiler_params=PARAMS,
        cost_estimate=pl.CostEstimate(flops=2 * 1024 * 2304 * 256, bytes_accessed=8 * 1024 * 1024, transcendentals=0),
        name="kernel_grads",
    )(acts)


def shift(value, axis, by):
    size = lax.axis_size(axis)
    return lax.ppermute(value, axis, [(i, i + by) for i in range(size) if 0 <= i + by < size])


def turn(value, axis, by):
    size = lax.axis_size(axis)
    return lax.ppermute(value, axis, [(i, (i + by) % size) for i in range(size)])


def around(value, by):
    return lax.ppermute(value, ("y", "core"), [(i, (i + by) % 8) for i in range(8)])


def unpack_kernel(meta, *refs):
    place = meta[2]
    for d in range(8):
        at = pl.multiple_of(lax.rem(place + 8 - d, 8) * 16, 16)
        refs[8][pl.ds(at, 16), :] = refs[d][:, 0:2 * C]
        refs[9][pl.ds(at, 16), :] = refs[d][:, 2 * C:4 * C]


def unpack(meta, back):
    return pl.pallas_call(
        unpack_kernel,
        out_shape=[jax.ShapeDtypeStruct((128, 2 * C), bf16)] * 2,
        in_specs=[SMEM] + [VMEM] * 8,
        out_specs=[VMEM] * 2,
        compiler_params=PARAMS,
        name="unpack",
    )(meta, *back)


def local(block_out, out_grad, weights):
    z, y, core, section = (lax.axis_index(a) for a in ("z", "y", "core", "section"))
    meta = jnp.stack([core, 8 * z, 2 * y + core, section, y]).astype(jnp.int32)

    own = lax.dynamic_index_in_dim(weights[0], core, 0, keepdims=False)
    part = turn(lax.dynamic_slice_in_dim(own, QUARTER * y, QUARTER, 0), "section", 2)
    one, three = turn(own, "section", -1), turn(own, "section", 1)

    tile = lax.all_to_all(make_pieces(block_out[0, 0], out_grad[0, 0]), ("y", "core"), 0, 0)
    far = (shift(tile[7, :WIDE], "z", 2), shift(tile[0, :WIDE], "z", -2))
    near = (shift(tile, "z", 1), shift(tile, "z", -1))
    quarters = [part] + [turn(part, "y", d) for d in (1, 2, 3)]

    far, near, one, three, quarters = lax.optimization_barrier((far, near, one, three, quarters))
    others = [turn(v, "core", 1) for v in (one, three, *quarters)]
    fields = (near[0], tile, near[1], *far)
    done, acts = blocks(meta, fields, (weights[0], one, others[0], three, others[1], *quarters, *others[2:]))

    back = [done[0]] + [around(done[d], d) for d in range(1, 8)]
    got = lax.all_to_all(acts, ("core", "section"), 0, 0)
    got, back = lax.optimization_barrier((got, back))
    grad = kernel_grads(got)
    restored, input_grad = unpack(meta, back)
    grad = lax.all_to_all(grad, "y", 0, 0).astype(f32).sum(axis=0).astype(bf16)
    grad = lax.all_to_all(grad, "z", 0, 0).astype(f32).sum(axis=0)
    here = lax.dynamic_slice_in_dim(grad, 36 * core, 36, 0)
    there = turn(lax.dynamic_slice_in_dim(grad, 36 * (1 - core), 36, 0), "core", 1)
    grad = jnp.where(core == 0, jnp.stack([here, there]), jnp.stack([there, here]))
    return restored[None, None], input_grad[None, None], (grad * (1.0 / math.sqrt(32768)))[None]


def solution(mesh):
    fine = Mesh(mesh.devices.reshape(8, 4, 2, 4), ("z", "y", "core", "section"))
    rows = ("z", "y", "core")
    spec = P("section", rows, None, None)
    return jax.shard_map(
        local,
        mesh=fine,
        in_specs=(spec, spec, P("section", None, None, None)),
        out_specs=(spec, spec, P("section", None, rows, None)),
        check_vma=False,
    )
```

```python
import math

import jax
import jax.numpy as jnp
from jax import lax
from jax.experimental import pallas as pl
from jax.experimental.pallas import tpu as pltpu
from jax.sharding import Mesh
from jax.sharding import PartitionSpec as P

C = 256
W = 32
WIDE = 48
BOTH = W + 16
PIECE = WIDE + 16 + 3 * BOTH
QUARTER = 576
SPAN = 18
VMEM = pl.BlockSpec(memory_space=pltpu.VMEM)
HBM = pl.BlockSpec(memory_space=pltpu.HBM)
ANY = pl.BlockSpec(memory_space=pl.ANY)
PARAMS = pltpu.CompilerParams(vmem_limit_bytes=24 * 1024 * 1024)
f32, bf16 = jnp.float32, jnp.bfloat16


def row_chunks(rows, most=12):
    count = -(-rows // most)
    base, extra = divmod(rows, count)
    out, at = [], 0
    for i in range(count):
        size = base + (1 if i < extra else 0)
        out.append((at, size))
        at += size
    return out


def pieces_kernel(field, cotangent, out, padded):
    padded[0:16] = jnp.zeros((16, 4 * C), f32)
    padded[144:160] = jnp.zeros((16, 4 * C), f32)
    padded[16:144, 0:2 * C] = field[...].astype(f32)
    padded[16:144, 2 * C:4 * C] = cotangent[...].astype(f32)
    for chip in range(4):
        piece = [padded[32 * chip:32 * chip + WIDE + 16, 0:C].astype(bf16)]
        for i in range(1, 4):
            piece.append(padded[32 * chip + 8:32 * chip + 8 + BOTH, i * C:(i + 1) * C].astype(bf16))
        piece = jnp.concatenate(piece, axis=0)
        out[2 * chip] = piece
        out[2 * chip + 1] = piece


def make_pieces(field, cotangent):
    return pl.pallas_call(
        pieces_kernel,
        out_shape=jax.ShapeDtypeStruct((8, PIECE, C), bf16),
        in_specs=[VMEM, VMEM],
        out_specs=VMEM,
        scratch_shapes=[pltpu.VMEM((160, 4 * C), f32)],
        compiler_params=PARAMS,
        name="pieces",
    )(field, cotangent)


def blocks_kernel(tile, beyond, beyond2, far, far2, held, first, first2, second, second2, quarters, quarters2,
                  done, acts, w, near, ends, s1a, s1b, s2a, s2b, s3, s4, t1a, t1b, n2a, n2b, packed, sent, sems):
    z, y, core, section = (lax.axis_index(a) for a in ("z", "y", "core", "section"))
    rowbase, place = 8 * z, 2 * y + core
    colbase = 16 * place

    loads = [pltpu.make_async_copy(src, dst, sems.at[12 + i]) for i, (src, dst) in enumerate((
        (beyond, near.at[core]), (beyond2, near.at[1 - core]), (far, ends.at[core]), (far2, ends.at[1 - core])))]
    for load in loads:
        load.start()

    def kernel_copy(k, src, part=()):
        return pltpu.make_async_copy(src, w.at[(k, *part)], sems.at[k])

    for k in (3, 2, 1, 0):
        ahead = lax.rem(k + 4 - section, 4)
        mine = 1 + 2 * core

        @pl.when(ahead == 0)
        def _():
            kernel_copy(k, held).start()

        @pl.when(ahead == mine)
        def _():
            kernel_copy(k, first, (0,)).start()
            kernel_copy(k, second, (1,)).start()

        @pl.when(ahead == 4 - mine)
        def _():
            kernel_copy(k, first2, (0,)).start()
            kernel_copy(k, second2, (1,)).start()

        @pl.when(ahead == 2)
        def _():
            for d in range(4):
                rows = pl.ds(QUARTER * d, QUARTER)
                kernel_copy(k, quarters.at[d], (core, rows)).start()
                kernel_copy(k, quarters2.at[d], (1 - core, rows)).start()

    def put(buf, at, mid, left, right):
        n = mid.shape[0]
        rows = slice(at * W, (at + n) * W)
        buf[rows, 0:C] = left.reshape(n * W, C).astype(bf16)
        buf[rows, C:2 * C] = mid.reshape(n * W, C).astype(bf16)
        buf[rows, 2 * C:3 * C] = right.reshape(n * W, C).astype(bf16)

    def spread(buf, at, value):
        n, wide = value.shape[0], value.shape[1]
        flat = value.reshape(n * wide, C)
        left = pltpu.roll(flat, 1, 0).reshape(n, wide, C)
        right = pltpu.roll(flat, n * wide - 1, 0).reshape(n, wide, C)
        cut = (wide - W) // 2
        put(buf, at, *(v[:, cut:cut + W] for v in (value, left, right)))

    def inside(a, n, halo):
        r = lax.broadcasted_iota(jnp.int32, (n, W, 1), 0) + (rowbase - halo + a)
        c = lax.broadcasted_iota(jnp.int32, (n, W, 1), 1) + (colbase - 8)
        return (r >= 0) & (r < 64) & (c >= 0) & (c < 128)

    def conv(buf, a, n, k, branch):
        acc = None
        for dr in range(3):
            d = jnp.dot(buf[(a + dr) * W:(a + dr + n) * W, :], w[k, branch, 768 * dr:768 * (dr + 1), :],
                        preferred_element_type=f32)
            acc = d if acc is None else acc + d
        return acc.reshape(n, W, C)

    def conv_t(buf, a, n, k, branch):
        acc = None
        for dr in range(3):
            for dc in range(3):
                tap = 3 * dr + dc
                d = lax.dot_general(buf[(a + 2 - dr) * W:(a + 2 - dr + n) * W, (2 - dc) * C:(3 - dc) * C],
                                    w[k, branch, 256 * tap:256 * (tap + 1), :],
                                    (((1,), (1,)), ((), ())), preferred_element_type=f32)
                acc = d if acc is None else acc + d
        return acc.reshape(n, W, C)

    def window(which, a, n, halo):
        lo, size = (0, WIDE) if which == 0 else (WIDE + 16 + (which - 1) * BOTH, W)
        cols = pl.ds(pl.multiple_of(lo + 16 * core, 16), size)
        parts, at = [], a - halo
        while at < a - halo + n:
            if at < -8 or at >= 16:
                part, took = ends[0 if at < 0 else 1, cols][None], 1
            elif 0 <= at < 8:
                took = min(a - halo + n, 8) - at
                part = tile[at:at + took, cols]
            else:
                side, base = (0, -8) if at < 0 else (1, 8)
                took = min(a - halo + n, base + 8) - at
                part = near[side, at - base:at - base + took, cols]
            parts.append(part.astype(f32))
            at += took
        return parts[0] if len(parts) == 1 else jnp.concatenate(parts, axis=0)

    def lanes(buf, a, n):
        return buf[a * W:(a + n) * W, C:2 * C].astype(f32).reshape(n, W, C)

    def finish(which, value, a, n, halo):
        lo, hi = max(a, halo), min(a + n, halo + 8)
        for i in range(lo, hi):
            at = lax.rem(i - halo + 8 - place, 8)
            done[at, :, which * C:(which + 1) * C] = value[i - a, 8:24].astype(bf16)

    for load in loads:
        load.wait()
    for a, n in row_chunks(26):
        spread(s1a, a, window(0, a, n, 9))
    for k, p in ((3, 8), (2, 6), (1, 4), (0, 2)):
        top, last = k == 3, k == 0
        s1, s1n = (s1a, s1b) if k % 2 else (s1b, s1a)
        s2, s2o = (s2a, s2b) if k % 2 else (s2b, s2a)
        t1n, t1o = (t1a, t1b) if k % 2 else (t1b, t1a)
        n2n, n2o = (n2a, n2b) if k % 2 else (n2b, n2a)

        def old_y2(a, n):
            return window(1, a, n, p) if top else lanes(s2o, a + 2, n)

        def old_g1(a, n):
            return window(2, a, n, p - 1) if top else t1o[a + 2:a + 2 + n].astype(f32)

        def old_g2(a, n):
            return window(3, a, n, p) if top else n2o[a:a + n].astype(f32)

        kernel_copy(k, held).wait()
        for a, n in row_chunks(8 + 2 * p):
            pre = conv(s1, a, n, k, 1)
            sig = jax.nn.sigmoid(pre)
            x2 = jnp.where(inside(a, n, p), old_y2(a, n) - pre * sig, 0.0)
            x2 = x2.astype(bf16).astype(f32)
            spread(s2, a, x2)
            if last:
                finish(1, x2, a, n, p)
            dg = old_g2(a, n) * (sig * (1.0 + pre * (1.0 - sig)))
            spread(s3, a, dg.astype(bf16).astype(f32))
        for a, n in row_chunks(6 + 2 * p):
            pre = conv(s2, a, n, k, 0)
            sig = jax.nn.sigmoid(pre)
            m = inside(a, n, p - 1)
            x1 = jnp.where(m, lanes(s1, a + 2, n) - pre * sig, 0.0)
            t1 = jnp.where(m, old_g1(a, n) + conv_t(s3, a, n, k, 1), 0.0)
            t1 = t1.astype(bf16).astype(f32)
            df = t1 * (sig * (1.0 + pre * (1.0 - sig)))
            spread(s4, a, df.astype(bf16).astype(f32))
            if last:
                finish(0, x1, a, n, p - 1)
                finish(2, t1, a, n, p - 1)
            else:
                spread(s1n, a, x1.astype(bf16).astype(f32))
                t1n[a:a + n] = t1.astype(bf16)
        for a, n in row_chunks(4 + 2 * p):
            n2 = jnp.where(inside(a, n, p - 2), old_g2(a + 2, n) + conv_t(s4, a, n, k, 0), 0.0)
            if last:
                finish(3, n2, a, n, p - 2)
            else:
                n2n[a:a + n] = n2.astype(bf16)

        for branch, src, h, delta, hd in ((0, s2, p, s4, p - 1), (1, s1, p + 1, s3, p)):
            for i in range(10):
                v = src[(h - 1 + i) * W:(h + i) * W, 0:C].astype(f32)
                packed[SPAN * i:SPAN * i + 24] = v[8:32]
            sent[4 * branch + k, 0:192] = packed[0:192].astype(bf16)
            d = lanes(delta, hd, 8)[:, 8:24]
            sent[4 * branch + k, 192:320] = d.reshape(128, C).astype(bf16)
            pltpu.make_async_copy(sent.at[4 * branch + k], acts.at[4 * branch + k], sems.at[4 + 4 * branch + k]).start()
    for i in range(8):
        pltpu.make_async_copy(sent.at[i], acts.at[i], sems.at[4 + i]).wait()


def blocks(fields, kernels):
    def spread(rows):
        return pltpu.VMEM((rows * W, 3 * C), bf16)

    def plain(rows):
        return pltpu.VMEM((rows, W, C), bf16)

    flops = sum(2 * 2304 * 256 * W * (4 * (8 + 2 * p) - 12) for p in (8, 6, 4, 2))
    return pl.pallas_call(
        blocks_kernel,
        out_shape=[jax.ShapeDtypeStruct((8, 16, 4 * C), bf16), jax.ShapeDtypeStruct((8, 320, C), bf16)],
        in_specs=[VMEM] + [ANY] * (4 + len(kernels)),
        out_specs=[VMEM, HBM],
        scratch_shapes=[pltpu.VMEM((4, 2, 2304, C), bf16), pltpu.VMEM((2, 8, PIECE, C), bf16), pltpu.VMEM((2, WIDE + 16, C), bf16),
                        spread(26), spread(22), spread(24), spread(20), spread(24), spread(22),
                        plain(22), plain(18), plain(20), plain(16),
                        pltpu.VMEM((192, C), f32), pltpu.VMEM((8, 320, C), bf16), pltpu.SemaphoreType.DMA((16,))],
        compiler_params=pltpu.CompilerParams(vmem_limit_bytes=56 * 1024 * 1024),
        cost_estimate=pl.CostEstimate(flops=flops, bytes_accessed=16 * 1024 * 1024, transcendentals=0),
        name="blocks",
    )(*fields, *kernels)


def grad_kernel(acts, out, lhs, packed, grad):
    for m in range(8):
        packed[0:192] = acts[m, 0:192].astype(f32)
        for i in range(10):
            for dc in range(3):
                v = packed[SPAN * i + dc:SPAN * i + dc + 16, :].astype(bf16)
                for dr in range(3):
                    if 0 <= i - dr < 8:
                        at, t = m * 128 + (i - dr) * 16, 3 * dr + dc
                        lhs[at:at + 16, t * C:(t + 1) * C] = v
    d = jnp.concatenate([acts[m, 192:320] for m in range(8)], axis=0)
    for t in range(9):
        grad[t * C:(t + 1) * C, :] = lax.dot_general(
            lhs[:, t * C:(t + 1) * C], d, (((0,), (0,)), ((), ())), preferred_element_type=f32)
    here = lax.axis_index("y")
    for z in range(8):
        for y in range(4):
            at = (4 * z + y) * 72
            out[lax.rem(y + 4 - here, 4), z] = grad[at:at + 72].astype(bf16)


def kernel_grads(acts):
    return pl.pallas_call(
        grad_kernel,
        out_shape=jax.ShapeDtypeStruct((4, 8, 72, C), bf16),
        in_specs=[VMEM],
        out_specs=VMEM,
        scratch_shapes=[pltpu.VMEM((1024, 2304), bf16), pltpu.VMEM((192, C), f32), pltpu.VMEM((2304, C), f32)],
        compiler_params=PARAMS,
        cost_estimate=pl.CostEstimate(flops=2 * 1024 * 2304 * 256, bytes_accessed=8 * 1024 * 1024, transcendentals=0),
        name="kernel_grads",
    )(acts)


def turn(value, axis, by):
    size = lax.axis_size(axis)
    return lax.ppermute(value, axis, [(i, (i + by) % size) for i in range(size)])


def apart(value, by):
    pairs = [(2 * i + c, 2 * (i + d) + c) for c, d in ((0, by), (1, -by)) for i in range(8) if 0 <= i + d < 8]
    return lax.ppermute(value, ("z", "core"), pairs)


def around(value, by):
    return lax.ppermute(value, ("y", "core"), [(i, (i + by) % 8) for i in range(8)])


def unpack_kernel(*refs):
    place = 2 * lax.axis_index("y") + lax.axis_index("core")
    for d in range(8):
        at = pl.multiple_of(lax.rem(place + 8 - d, 8) * 16, 16)
        refs[8][pl.ds(at, 16), :] = refs[d][:, 0:2 * C]
        refs[9][pl.ds(at, 16), :] = refs[d][:, 2 * C:4 * C]


def unpack(back):
    return pl.pallas_call(
        unpack_kernel,
        out_shape=[jax.ShapeDtypeStruct((128, 2 * C), bf16)] * 2,
        in_specs=[VMEM] * 8,
        out_specs=[VMEM] * 2,
        compiler_params=PARAMS,
        name="unpack",
    )(*back)


def local(block_out, out_grad, weights):
    y, core = lax.axis_index("y"), lax.axis_index("core")

    part = lax.dynamic_slice(weights[0], (core, QUARTER * y, 0), (1, QUARTER, C))[0]
    part = turn(part, "section", 2)
    beside = [lax.ppermute(weights[0, i], ("core", "section"),
                           [(4 * c + i, 4 * c + (i + (-1, 1)[c]) % 4) for c in range(2) for i in range(4)])
              for i in range(2)]

    tile = lax.all_to_all(make_pieces(block_out[0, 0], out_grad[0, 0]), ("y", "core"), 0, 0)
    part = jnp.broadcast_to(part[None], (4, QUARTER, C))
    tile, part = lax.optimization_barrier((tile, part))
    beyond = apart(tile, 1)
    far = apart(jnp.where(core == 0, tile[7, :WIDE + 16], tile[0, :WIDE + 16]), 2)
    quarters = lax.all_to_all(part, "y", 0, 0)

    beyond, far, beside, quarters = lax.optimization_barrier((beyond, far, beside, quarters))
    moved = [v for m in (*beside, quarters) for v in (m, turn(m, "core", 1))]
    fields = (tile, beyond, turn(beyond, "core", 1), far, turn(far, "core", 1))
    done, acts = blocks(fields, (weights[0], *moved))

    back = [done[0]] + [around(done[d], d) for d in range(1, 8)]
    got = lax.all_to_all(acts, ("core", "section"), 0, 0)
    got, back = lax.optimization_barrier((got, back))
    grad = kernel_grads(got)
    restored, input_grad = unpack(back)
    terms = [grad[0]] + [turn(grad[d], "y", d) for d in (1, 2, 3)]
    grad = sum(t.astype(f32) for t in terms).astype(bf16)
    grad = lax.all_to_all(grad, "z", 0, 0).astype(f32).sum(axis=0)
    here = lax.dynamic_slice_in_dim(grad, 36 * core, 36, 0)
    there = turn(lax.dynamic_slice_in_dim(grad, 36 * (1 - core), 36, 0), "core", 1)
    grad = jnp.where(core == 0, jnp.stack([here, there]), jnp.stack([there, here]))
    return restored[None, None], input_grad[None, None], (grad * (1.0 / math.sqrt(32768)))[None]


def solution(mesh):
    fine = Mesh(mesh.devices.reshape(8, 4, 2, 4), ("z", "y", "core", "section"))
    rows = ("z", "y", "core")
    spec = P("section", rows, None, None)
    return jax.shard_map(
        local,
        mesh=fine,
        in_specs=(spec, spec, P("section", None, None, None)),
        out_specs=(spec, spec, P("section", None, rows, None)),
        check_vma=False,
    )
```

```python
import math

import jax
import jax.numpy as jnp
from jax import lax
from jax.experimental import pallas as pl
from jax.experimental.pallas import tpu as pltpu
from jax.sharding import Mesh
from jax.sharding import PartitionSpec as P

C = 256
W = 32
WIDE = 48
BOTH = W + 16
PIECE = WIDE + 16 + 3 * BOTH
QUARTER = 576
SPAN = 18
VMEM = pl.BlockSpec(memory_space=pltpu.VMEM)
HBM = pl.BlockSpec(memory_space=pltpu.HBM)
ANY = pl.BlockSpec(memory_space=pl.ANY)
PARAMS = pltpu.CompilerParams(vmem_limit_bytes=24 * 1024 * 1024)
f32, bf16 = jnp.float32, jnp.bfloat16


def row_chunks(rows, most=12):
    count = -(-rows // most)
    base, extra = divmod(rows, count)
    out, at = [], 0
    for i in range(count):
        size = base + (1 if i < extra else 0)
        out.append((at, size))
        at += size
    return out


def pieces_kernel(field, cotangent, held, out, part, padded, sem):
    at = pl.multiple_of(QUARTER * lax.axis_index("y"), QUARTER)
    quarter = pltpu.make_async_copy(held.at[lax.axis_index("core"), pl.ds(at, QUARTER)], part, sem)
    quarter.start()
    padded[0:16] = jnp.zeros((16, 4 * C), f32)
    padded[144:160] = jnp.zeros((16, 4 * C), f32)
    padded[16:144, 0:2 * C] = field[...].astype(f32)
    padded[16:144, 2 * C:4 * C] = cotangent[...].astype(f32)
    for chip in range(4):
        piece = [padded[32 * chip:32 * chip + WIDE + 16, 0:C].astype(bf16)]
        for i in range(1, 4):
            piece.append(padded[32 * chip + 8:32 * chip + 8 + BOTH, i * C:(i + 1) * C].astype(bf16))
        piece = jnp.concatenate(piece, axis=0)
        out[2 * chip] = piece
        out[2 * chip + 1] = piece
    quarter.wait()


def make_pieces(field, cotangent, held):
    return pl.pallas_call(
        pieces_kernel,
        out_shape=[jax.ShapeDtypeStruct((8, PIECE, C), bf16), jax.ShapeDtypeStruct((QUARTER, C), bf16)],
        in_specs=[VMEM, VMEM, ANY],
        out_specs=[VMEM, VMEM],
        scratch_shapes=[pltpu.VMEM((160, 4 * C), f32), pltpu.SemaphoreType.DMA],
        compiler_params=PARAMS,
        name="pieces",
    )(field, cotangent, held)


def repeat_kernel(part, out):
    for i in range(4):
        out[i] = part[...]


def repeat(part):
    return pl.pallas_call(
        repeat_kernel,
        out_shape=jax.ShapeDtypeStruct((4, QUARTER, C), bf16),
        in_specs=[VMEM],
        out_specs=VMEM,
        compiler_params=PARAMS,
        name="repeat",
    )(part)


def blocks_kernel(tile, beyond, beyond2, far, far2, held, first, first2, second, second2, quarters, quarters2,
                  done, acts, w, near, ends, s1a, s1b, s2a, s2b, s3, s4, t1a, t1b, n2a, n2b, packed, sent, sems):
    z, y, core, section = (lax.axis_index(a) for a in ("z", "y", "core", "section"))
    rowbase, place = 8 * z, 2 * y + core
    colbase = 16 * place

    loads = [pltpu.make_async_copy(src, dst, sems.at[12 + i]) for i, (src, dst) in enumerate((
        (beyond, near.at[core]), (beyond2, near.at[1 - core]), (far, ends.at[core]), (far2, ends.at[1 - core])))]
    for load in loads:
        load.start()

    def kernel_copy(k, src, part=()):
        return pltpu.make_async_copy(src, w.at[(k, *part)], sems.at[k])

    for k in (3, 2, 1, 0):
        ahead = lax.rem(k + 4 - section, 4)
        mine = 1 + 2 * core

        @pl.when(ahead == 0)
        def _():
            kernel_copy(k, held).start()

        @pl.when(ahead == mine)
        def _():
            kernel_copy(k, first, (0,)).start()
            kernel_copy(k, second, (1,)).start()

        @pl.when(ahead == 4 - mine)
        def _():
            kernel_copy(k, first2, (0,)).start()
            kernel_copy(k, second2, (1,)).start()

        @pl.when(ahead == 2)
        def _():
            for d in range(4):
                rows = pl.ds(QUARTER * d, QUARTER)
                kernel_copy(k, quarters.at[d], (core, rows)).start()
                kernel_copy(k, quarters2.at[d], (1 - core, rows)).start()

    def put(buf, at, mid, left, right):
        n = mid.shape[0]
        rows = slice(at * W, (at + n) * W)
        buf[rows, 0:C] = left.reshape(n * W, C).astype(bf16)
        buf[rows, C:2 * C] = mid.reshape(n * W, C).astype(bf16)
        buf[rows, 2 * C:3 * C] = right.reshape(n * W, C).astype(bf16)

    def spread(buf, at, value):
        n, wide = value.shape[0], value.shape[1]
        flat = value.reshape(n * wide, C)
        left = pltpu.roll(flat, 1, 0).reshape(n, wide, C)
        right = pltpu.roll(flat, n * wide - 1, 0).reshape(n, wide, C)
        cut = (wide - W) // 2
        put(buf, at, *(v[:, cut:cut + W] for v in (value, left, right)))

    def inside(a, n, halo):
        r = lax.broadcasted_iota(jnp.int32, (n, W, 1), 0) + (rowbase - halo + a)
        c = lax.broadcasted_iota(jnp.int32, (n, W, 1), 1) + (colbase - 8)
        return (r >= 0) & (r < 64) & (c >= 0) & (c < 128)

    def conv(buf, a, n, k, branch):
        acc = None
        for dr in range(3):
            d = jnp.dot(buf[(a + dr) * W:(a + dr + n) * W, :], w[k, branch, 768 * dr:768 * (dr + 1), :],
                        preferred_element_type=f32)
            acc = d if acc is None else acc + d
        return acc.reshape(n, W, C)

    def conv_t(buf, a, n, k, branch):
        acc = None
        for dr in range(3):
            for dc in range(3):
                tap = 3 * dr + dc
                d = lax.dot_general(buf[(a + 2 - dr) * W:(a + 2 - dr + n) * W, (2 - dc) * C:(3 - dc) * C],
                                    w[k, branch, 256 * tap:256 * (tap + 1), :],
                                    (((1,), (1,)), ((), ())), preferred_element_type=f32)
                acc = d if acc is None else acc + d
        return acc.reshape(n, W, C)

    def window(which, a, n, halo):
        lo, size = (0, WIDE) if which == 0 else (WIDE + 16 + (which - 1) * BOTH, W)
        cols = pl.ds(pl.multiple_of(lo + 16 * core, 16), size)
        parts, at = [], a - halo
        while at < a - halo + n:
            if at < -8 or at >= 16:
                part, took = ends[0 if at < 0 else 1, cols][None], 1
            elif 0 <= at < 8:
                took = min(a - halo + n, 8) - at
                part = tile[at:at + took, cols]
            else:
                side, base = (0, -8) if at < 0 else (1, 8)
                took = min(a - halo + n, base + 8) - at
                part = near[side, at - base:at - base + took, cols]
            parts.append(part.astype(f32))
            at += took
        return parts[0] if len(parts) == 1 else jnp.concatenate(parts, axis=0)

    def lanes(buf, a, n):
        return buf[a * W:(a + n) * W, C:2 * C].astype(f32).reshape(n, W, C)

    def finish(which, value, a, n, halo):
        lo, hi = max(a, halo), min(a + n, halo + 8)
        for i in range(lo, hi):
            at = lax.rem(i - halo + 8 - place, 8)
            done[at, :, which * C:(which + 1) * C] = value[i - a, 8:24].astype(bf16)

    for load in loads:
        load.wait()
    for a, n in row_chunks(26):
        spread(s1a, a, window(0, a, n, 9))
    for k, p in ((3, 8), (2, 6), (1, 4), (0, 2)):
        top, last = k == 3, k == 0
        s1, s1n = (s1a, s1b) if k % 2 else (s1b, s1a)
        s2, s2o = (s2a, s2b) if k % 2 else (s2b, s2a)
        t1n, t1o = (t1a, t1b) if k % 2 else (t1b, t1a)
        n2n, n2o = (n2a, n2b) if k % 2 else (n2b, n2a)

        def old_y2(a, n):
            return window(1, a, n, p) if top else lanes(s2o, a + 2, n)

        def old_g1(a, n):
            return window(2, a, n, p - 1) if top else t1o[a + 2:a + 2 + n].astype(f32)

        def old_g2(a, n):
            return window(3, a, n, p) if top else n2o[a:a + n].astype(f32)

        kernel_copy(k, held).wait()
        for a, n in row_chunks(8 + 2 * p):
            pre = conv(s1, a, n, k, 1)
            sig = jax.nn.sigmoid(pre)
            x2 = jnp.where(inside(a, n, p), old_y2(a, n) - pre * sig, 0.0)
            x2 = x2.astype(bf16).astype(f32)
            spread(s2, a, x2)
            if last:
                finish(1, x2, a, n, p)
            dg = old_g2(a, n) * (sig * (1.0 + pre * (1.0 - sig)))
            spread(s3, a, dg.astype(bf16).astype(f32))
        for a, n in row_chunks(6 + 2 * p):
            pre = conv(s2, a, n, k, 0)
            sig = jax.nn.sigmoid(pre)
            m = inside(a, n, p - 1)
            x1 = jnp.where(m, lanes(s1, a + 2, n) - pre * sig, 0.0)
            t1 = jnp.where(m, old_g1(a, n) + conv_t(s3, a, n, k, 1), 0.0)
            t1 = t1.astype(bf16).astype(f32)
            df = t1 * (sig * (1.0 + pre * (1.0 - sig)))
            spread(s4, a, df.astype(bf16).astype(f32))
            if last:
                finish(0, x1, a, n, p - 1)
                finish(2, t1, a, n, p - 1)
            else:
                spread(s1n, a, x1.astype(bf16).astype(f32))
                t1n[a:a + n] = t1.astype(bf16)
        for a, n in row_chunks(4 + 2 * p):
            n2 = jnp.where(inside(a, n, p - 2), old_g2(a + 2, n) + conv_t(s4, a, n, k, 0), 0.0)
            if last:
                finish(3, n2, a, n, p - 2)
            else:
                n2n[a:a + n] = n2.astype(bf16)

        for branch, src, h, delta, hd in ((0, s2, p, s4, p - 1), (1, s1, p + 1, s3, p)):
            for i in range(10):
                v = src[(h - 1 + i) * W:(h + i) * W, 0:C].astype(f32)
                packed[SPAN * i:SPAN * i + 24] = v[8:32]
            sent[4 * branch + k, 0:192] = packed[0:192].astype(bf16)
            d = lanes(delta, hd, 8)[:, 8:24]
            sent[4 * branch + k, 192:320] = d.reshape(128, C).astype(bf16)
            pltpu.make_async_copy(sent.at[4 * branch + k], acts.at[4 * branch + k], sems.at[4 + 4 * branch + k]).start()
    for i in range(8):
        pltpu.make_async_copy(sent.at[i], acts.at[i], sems.at[4 + i]).wait()


def blocks(fields, kernels):
    def spread(rows):
        return pltpu.VMEM((rows * W, 3 * C), bf16)

    def plain(rows):
        return pltpu.VMEM((rows, W, C), bf16)

    flops = sum(2 * 2304 * 256 * W * (4 * (8 + 2 * p) - 12) for p in (8, 6, 4, 2))
    return pl.pallas_call(
        blocks_kernel,
        out_shape=[jax.ShapeDtypeStruct((8, 16, 4 * C), bf16), jax.ShapeDtypeStruct((8, 320, C), bf16)],
        in_specs=[VMEM] + [ANY] * (4 + len(kernels)),
        out_specs=[VMEM, HBM],
        scratch_shapes=[pltpu.VMEM((4, 2, 2304, C), bf16), pltpu.VMEM((2, 8, PIECE, C), bf16), pltpu.VMEM((2, WIDE + 16, C), bf16),
                        spread(26), spread(22), spread(24), spread(20), spread(24), spread(22),
                        plain(22), plain(18), plain(20), plain(16),
                        pltpu.VMEM((192, C), f32), pltpu.VMEM((8, 320, C), bf16), pltpu.SemaphoreType.DMA((16,))],
        compiler_params=pltpu.CompilerParams(vmem_limit_bytes=56 * 1024 * 1024),
        cost_estimate=pl.CostEstimate(flops=flops, bytes_accessed=16 * 1024 * 1024, transcendentals=0),
        name="blocks",
    )(*fields, *kernels)


def grad_kernel(acts, out, lhs, packed, grad):
    for m in range(8):
        packed[0:192] = acts[m, 0:192].astype(f32)
        for i in range(10):
            for dc in range(3):
                v = packed[SPAN * i + dc:SPAN * i + dc + 16, :].astype(bf16)
                for dr in range(3):
                    if 0 <= i - dr < 8:
                        at, t = m * 128 + (i - dr) * 16, 3 * dr + dc
                        lhs[at:at + 16, t * C:(t + 1) * C] = v
    d = jnp.concatenate([acts[m, 192:320] for m in range(8)], axis=0)
    for t in range(9):
        grad[t * C:(t + 1) * C, :] = lax.dot_general(
            lhs[:, t * C:(t + 1) * C], d, (((0,), (0,)), ((), ())), preferred_element_type=f32)
    here = lax.axis_index("y")
    for z in range(8):
        for y in range(4):
            at = (4 * z + y) * 72
            out[lax.rem(y + 4 - here, 4), z] = grad[at:at + 72].astype(bf16)


def kernel_grads(acts):
    return pl.pallas_call(
        grad_kernel,
        out_shape=jax.ShapeDtypeStruct((4, 8, 72, C), bf16),
        in_specs=[VMEM],
        out_specs=VMEM,
        scratch_shapes=[pltpu.VMEM((1024, 2304), bf16), pltpu.VMEM((192, C), f32), pltpu.VMEM((2304, C), f32)],
        compiler_params=PARAMS,
        cost_estimate=pl.CostEstimate(flops=2 * 1024 * 2304 * 256, bytes_accessed=8 * 1024 * 1024, transcendentals=0),
        name="kernel_grads",
    )(acts)


def turn(value, axis, by):
    size = lax.axis_size(axis)
    return lax.ppermute(value, axis, [(i, (i + by) % size) for i in range(size)])


def apart(value, by):
    pairs = [(2 * i + c, 2 * (i + d) + c) for c, d in ((0, by), (1, -by)) for i in range(8) if 0 <= i + d < 8]
    return lax.ppermute(value, ("z", "core"), pairs)


def around(value, by):
    return lax.ppermute(value, ("y", "core"), [(i, (i + by) % 8) for i in range(8)])


def unpack_kernel(*refs):
    place = 2 * lax.axis_index("y") + lax.axis_index("core")
    for d in range(8):
        at = pl.multiple_of(lax.rem(place + 8 - d, 8) * 16, 16)
        refs[8][pl.ds(at, 16), :] = refs[d][:, 0:2 * C]
        refs[9][pl.ds(at, 16), :] = refs[d][:, 2 * C:4 * C]


def unpack(back):
    return pl.pallas_call(
        unpack_kernel,
        out_shape=[jax.ShapeDtypeStruct((128, 2 * C), bf16)] * 2,
        in_specs=[VMEM] * 8,
        out_specs=[VMEM] * 2,
        compiler_params=PARAMS,
        name="unpack",
    )(*back)


def local(block_out, out_grad, weights):
    core = lax.axis_index("core")

    pieces, part = make_pieces(block_out[0, 0], out_grad[0, 0], weights[0])
    part = turn(part, "section", 2)
    beside = [lax.ppermute(weights[0, i], ("core", "section"),
                           [(4 * c + i, 4 * c + (i + (-1, 1)[c]) % 4) for c in range(2) for i in range(4)])
              for i in range(2)]

    tile = lax.all_to_all(pieces, ("y", "core"), 0, 0)
    part = repeat(part)
    tile, part = lax.optimization_barrier((tile, part))
    beyond = apart(tile, 1)
    far = apart(jnp.where(core == 0, tile[7, :WIDE + 16], tile[0, :WIDE + 16]), 2)
    quarters = lax.all_to_all(part, "y", 0, 0)

    beyond, far, beside, quarters = lax.optimization_barrier((beyond, far, beside, quarters))
    moved = [v for m in (*beside, quarters) for v in (m, turn(m, "core", 1))]
    fields = (tile, beyond, turn(beyond, "core", 1), far, turn(far, "core", 1))
    done, acts = blocks(fields, (weights[0], *moved))

    back = [done[0]] + [around(done[d], d) for d in range(1, 8)]
    got = lax.all_to_all(acts, ("core", "section"), 0, 0)
    got, back = lax.optimization_barrier((got, back))
    grad = kernel_grads(got)
    restored, input_grad = unpack(back)
    terms = [grad[0]] + [turn(grad[d], "y", d) for d in (1, 2, 3)]
    grad = sum(t.astype(f32) for t in terms).astype(bf16)
    grad = lax.all_to_all(grad, "z", 0, 0).astype(f32).sum(axis=0)
    here = lax.dynamic_slice_in_dim(grad, 36 * core, 36, 0)
    there = turn(lax.dynamic_slice_in_dim(grad, 36 * (1 - core), 36, 0), "core", 1)
    grad = jnp.where(core == 0, jnp.stack([here, there]), jnp.stack([there, here]))
    return restored[None, None], input_grad[None, None], (grad * (1.0 / math.sqrt(32768)))[None]


def solution(mesh):
    fine = Mesh(mesh.devices.reshape(8, 4, 2, 4), ("z", "y", "core", "section"))
    rows = ("z", "y", "core")
    spec = P("section", rows, None, None)
    return jax.shard_map(
        local,
        mesh=fine,
        in_specs=(spec, spec, P("section", None, None, None)),
        out_specs=(spec, spec, P("section", None, rows, None)),
        check_vma=False,
    )
```

```python
import math

import jax
import jax.numpy as jnp
from jax import lax
from jax.experimental import pallas as pl
from jax.experimental.pallas import tpu as pltpu
from jax.sharding import Mesh
from jax.sharding import PartitionSpec as P

C = 256
W = 32
WIDE = 48
BOTH = W + 16
PIECE = WIDE + 16 + 3 * BOTH
QUARTER = 576
SPAN = 18
VMEM = pl.BlockSpec(memory_space=pltpu.VMEM)
HBM = pl.BlockSpec(memory_space=pltpu.HBM)
ANY = pl.BlockSpec(memory_space=pl.ANY)
PARAMS = pltpu.CompilerParams(vmem_limit_bytes=24 * 1024 * 1024)
f32, bf16 = jnp.float32, jnp.bfloat16


def row_chunks(rows, most=12):
    count = -(-rows // most)
    base, extra = divmod(rows, count)
    out, at = [], 0
    for i in range(count):
        size = base + (1 if i < extra else 0)
        out.append((at, size))
        at += size
    return out


def pieces_kernel(field, cotangent, held, out, part, padded, sem):
    at = pl.multiple_of(QUARTER * lax.axis_index("y"), QUARTER)
    quarter = pltpu.make_async_copy(held.at[lax.axis_index("core"), pl.ds(at, QUARTER)], part, sem)
    quarter.start()
    padded[0:16] = jnp.zeros((16, 4 * C), f32)
    padded[144:160] = jnp.zeros((16, 4 * C), f32)
    padded[16:144, 0:2 * C] = field[...].astype(f32)
    padded[16:144, 2 * C:4 * C] = cotangent[...].astype(f32)
    for chip in range(4):
        piece = [padded[32 * chip:32 * chip + WIDE + 16, 0:C].astype(bf16)]
        for i in range(1, 4):
            piece.append(padded[32 * chip + 8:32 * chip + 8 + BOTH, i * C:(i + 1) * C].astype(bf16))
        piece = jnp.concatenate(piece, axis=0)
        out[2 * chip] = piece
        out[2 * chip + 1] = piece
    quarter.wait()


def make_pieces(field, cotangent, held):
    return pl.pallas_call(
        pieces_kernel,
        out_shape=[jax.ShapeDtypeStruct((8, PIECE, C), bf16), jax.ShapeDtypeStruct((QUARTER, C), bf16)],
        in_specs=[VMEM, VMEM, ANY],
        out_specs=[VMEM, VMEM],
        scratch_shapes=[pltpu.VMEM((160, 4 * C), f32), pltpu.SemaphoreType.DMA],
        compiler_params=PARAMS,
        name="pieces",
    )(field, cotangent, held)


def repeat_kernel(part, out):
    for i in range(4):
        out[i] = part[...]


def repeat(part):
    return pl.pallas_call(
        repeat_kernel,
        out_shape=jax.ShapeDtypeStruct((4, QUARTER, C), bf16),
        in_specs=[VMEM],
        out_specs=VMEM,
        compiler_params=PARAMS,
        name="repeat",
    )(part)


def blocks_kernel(tile, beyond, beyond2, far, far2, held, first, first2, second, second2, quarters, quarters2,
                  done, acts, w, near, ends, s1a, s1b, s2a, s2b, s3, s4, t1a, t1b, n2a, n2b, packed, sent, sems):
    z, y, core, section = (lax.axis_index(a) for a in ("z", "y", "core", "section"))
    rowbase, place = 8 * z, 2 * y + core
    colbase = 16 * place

    loads = [pltpu.make_async_copy(src, dst, sems.at[12 + i]) for i, (src, dst) in enumerate((
        (beyond, near.at[core]), (beyond2, near.at[1 - core]), (far, ends.at[core]), (far2, ends.at[1 - core])))]
    for load in loads:
        load.start()

    def kernel_copy(k, src, part=()):
        return pltpu.make_async_copy(src, w.at[(k, *part)], sems.at[k])

    for k in (3, 2, 1, 0):
        ahead = lax.rem(k + 4 - section, 4)
        mine = 1 + 2 * core

        @pl.when(ahead == 0)
        def _():
            kernel_copy(k, held).start()

        @pl.when(ahead == mine)
        def _():
            kernel_copy(k, first, (0,)).start()
            kernel_copy(k, second, (1,)).start()

        @pl.when(ahead == 4 - mine)
        def _():
            kernel_copy(k, first2, (0,)).start()
            kernel_copy(k, second2, (1,)).start()

        @pl.when(ahead == 2)
        def _():
            for d in range(4):
                rows = pl.ds(QUARTER * d, QUARTER)
                kernel_copy(k, quarters.at[d], (core, rows)).start()
                kernel_copy(k, quarters2.at[d], (1 - core, rows)).start()

    def put(buf, at, mid, left, right):
        n = mid.shape[0]
        rows = slice(at * W, (at + n) * W)
        buf[rows, 0:C] = left.reshape(n * W, C).astype(bf16)
        buf[rows, C:2 * C] = mid.reshape(n * W, C).astype(bf16)
        buf[rows, 2 * C:3 * C] = right.reshape(n * W, C).astype(bf16)

    def spread(buf, at, value):
        n, wide = value.shape[0], value.shape[1]
        flat = value.reshape(n * wide, C)
        left = pltpu.roll(flat, 1, 0).reshape(n, wide, C)
        right = pltpu.roll(flat, n * wide - 1, 0).reshape(n, wide, C)
        cut = (wide - W) // 2
        put(buf, at, *(v[:, cut:cut + W] for v in (value, left, right)))

    def inside(a, n, halo):
        r = lax.broadcasted_iota(jnp.int32, (n, W, 1), 0) + (rowbase - halo + a)
        c = lax.broadcasted_iota(jnp.int32, (n, W, 1), 1) + (colbase - 8)
        return (r >= 0) & (r < 64) & (c >= 0) & (c < 128)

    def conv(buf, a, n, k, branch):
        acc = None
        for dr in range(3):
            d = jnp.dot(buf[(a + dr) * W:(a + dr + n) * W, :], w[k, branch, 768 * dr:768 * (dr + 1), :],
                        preferred_element_type=f32)
            acc = d if acc is None else acc + d
        return acc.reshape(n, W, C)

    def conv_t(buf, a, n, k, branch):
        acc = None
        for dr in range(3):
            for dc in range(3):
                tap = 3 * dr + dc
                d = lax.dot_general(buf[(a + 2 - dr) * W:(a + 2 - dr + n) * W, (2 - dc) * C:(3 - dc) * C],
                                    w[k, branch, 256 * tap:256 * (tap + 1), :],
                                    (((1,), (1,)), ((), ())), preferred_element_type=f32)
                acc = d if acc is None else acc + d
        return acc.reshape(n, W, C)

    def window(which, a, n, halo):
        lo, size = (0, WIDE) if which == 0 else (WIDE + 16 + (which - 1) * BOTH, W)
        cols = pl.ds(pl.multiple_of(lo + 16 * core, 16), size)
        parts, at = [], a - halo
        while at < a - halo + n:
            if at < -8 or at >= 16:
                part, took = ends[0 if at < 0 else 1, cols][None], 1
            elif 0 <= at < 8:
                took = min(a - halo + n, 8) - at
                part = tile[at:at + took, cols]
            else:
                side, base = (0, -8) if at < 0 else (1, 8)
                took = min(a - halo + n, base + 8) - at
                part = near[side, at - base:at - base + took, cols]
            parts.append(part.astype(f32))
            at += took
        return parts[0] if len(parts) == 1 else jnp.concatenate(parts, axis=0)

    def lanes(buf, a, n):
        return buf[a * W:(a + n) * W, C:2 * C].astype(f32).reshape(n, W, C)

    def finish(which, value, a, n, halo):
        lo, hi = max(a, halo), min(a + n, halo + 8)
        for i in range(lo, hi):
            at = lax.rem(i - halo + 8 - place, 8)
            done[at, :, which * C:(which + 1) * C] = value[i - a, 8:24].astype(bf16)

    for load in loads:
        load.wait()
    for a, n in row_chunks(26):
        spread(s1a, a, window(0, a, n, 9))
    for k, p in ((3, 8), (2, 6), (1, 4), (0, 2)):
        top, last = k == 3, k == 0
        s1, s1n = (s1a, s1b) if k % 2 else (s1b, s1a)
        s2, s2o = (s2a, s2b) if k % 2 else (s2b, s2a)
        t1n, t1o = (t1a, t1b) if k % 2 else (t1b, t1a)
        n2n, n2o = (n2a, n2b) if k % 2 else (n2b, n2a)

        def old_y2(a, n):
            return window(1, a, n, p) if top else lanes(s2o, a + 2, n)

        def old_g1(a, n):
            return window(2, a, n, p - 1) if top else t1o[a + 2:a + 2 + n].astype(f32)

        def old_g2(a, n):
            return window(3, a, n, p) if top else n2o[a:a + n].astype(f32)

        kernel_copy(k, held).wait()
        for a, n in row_chunks(8 + 2 * p):
            pre = conv(s1, a, n, k, 1)
            sig = jax.nn.sigmoid(pre)
            x2 = jnp.where(inside(a, n, p), old_y2(a, n) - pre * sig, 0.0)
            x2 = x2.astype(bf16).astype(f32)
            spread(s2, a, x2)
            if last:
                finish(1, x2, a, n, p)
            dg = old_g2(a, n) * (sig * (1.0 + pre * (1.0 - sig)))
            spread(s3, a, dg.astype(bf16).astype(f32))
        for a, n in row_chunks(6 + 2 * p):
            pre = conv(s2, a, n, k, 0)
            sig = jax.nn.sigmoid(pre)
            m = inside(a, n, p - 1)
            x1 = jnp.where(m, lanes(s1, a + 2, n) - pre * sig, 0.0)
            t1 = jnp.where(m, old_g1(a, n) + conv_t(s3, a, n, k, 1), 0.0)
            t1 = t1.astype(bf16).astype(f32)
            df = t1 * (sig * (1.0 + pre * (1.0 - sig)))
            spread(s4, a, df.astype(bf16).astype(f32))
            if last:
                finish(0, x1, a, n, p - 1)
                finish(2, t1, a, n, p - 1)
            else:
                spread(s1n, a, x1.astype(bf16).astype(f32))
                t1n[a:a + n] = t1.astype(bf16)
        for a, n in row_chunks(4 + 2 * p):
            n2 = jnp.where(inside(a, n, p - 2), old_g2(a + 2, n) + conv_t(s4, a, n, k, 0), 0.0)
            if last:
                finish(3, n2, a, n, p - 2)
            else:
                n2n[a:a + n] = n2.astype(bf16)

        for branch, src, h, delta, hd in ((0, s2, p, s4, p - 1), (1, s1, p + 1, s3, p)):
            for i in range(10):
                v = src[(h - 1 + i) * W:(h + i) * W, 0:C].astype(f32)
                packed[SPAN * i:SPAN * i + 24] = v[8:32]
            sent[4 * branch + k, 0:192] = packed[0:192].astype(bf16)
            d = lanes(delta, hd, 8)[:, 8:24]
            sent[4 * branch + k, 192:320] = d.reshape(128, C).astype(bf16)
            pltpu.make_async_copy(sent.at[4 * branch + k], acts.at[4 * branch + k], sems.at[4 + 4 * branch + k]).start()
    for i in range(8):
        pltpu.make_async_copy(sent.at[i], acts.at[i], sems.at[4 + i]).wait()


def blocks(fields, kernels):
    def spread(rows):
        return pltpu.VMEM((rows * W, 3 * C), bf16)

    def plain(rows):
        return pltpu.VMEM((rows, W, C), bf16)

    flops = sum(2 * 2304 * 256 * W * (4 * (8 + 2 * p) - 12) for p in (8, 6, 4, 2))
    return pl.pallas_call(
        blocks_kernel,
        out_shape=[jax.ShapeDtypeStruct((8, 16, 4 * C), bf16), jax.ShapeDtypeStruct((8, 320, C), bf16)],
        in_specs=[VMEM] + [ANY] * (4 + len(kernels)),
        out_specs=[VMEM, HBM],
        scratch_shapes=[pltpu.VMEM((4, 2, 2304, C), bf16), pltpu.VMEM((2, 8, PIECE, C), bf16), pltpu.VMEM((2, WIDE + 16, C), bf16),
                        spread(26), spread(22), spread(24), spread(20), spread(24), spread(22),
                        plain(22), plain(18), plain(20), plain(16),
                        pltpu.VMEM((192, C), f32), pltpu.VMEM((8, 320, C), bf16), pltpu.SemaphoreType.DMA((16,))],
        compiler_params=pltpu.CompilerParams(vmem_limit_bytes=44 * 1024 * 1024),
        cost_estimate=pl.CostEstimate(flops=flops, bytes_accessed=16 * 1024 * 1024, transcendentals=0),
        name="blocks",
    )(*fields, *kernels)


def grad_kernel(acts, out, lhs, packed, grad):
    for m in range(8):
        packed[0:192] = acts[m, 0:192].astype(f32)
        for i in range(10):
            for dc in range(3):
                v = packed[SPAN * i + dc:SPAN * i + dc + 16, :].astype(bf16)
                for dr in range(3):
                    if 0 <= i - dr < 8:
                        at, t = m * 128 + (i - dr) * 16, 3 * dr + dc
                        lhs[at:at + 16, t * C:(t + 1) * C] = v
    d = jnp.concatenate([acts[m, 192:320] for m in range(8)], axis=0)
    for t in range(9):
        grad[t * C:(t + 1) * C, :] = lax.dot_general(
            lhs[:, t * C:(t + 1) * C], d, (((0,), (0,)), ((), ())), preferred_element_type=f32)
    here = lax.axis_index("y")
    for z in range(8):
        for y in range(4):
            at = (4 * z + y) * 72
            out[lax.rem(y + 4 - here, 4), z] = grad[at:at + 72].astype(bf16)


def kernel_grads(acts):
    return pl.pallas_call(
        grad_kernel,
        out_shape=jax.ShapeDtypeStruct((4, 8, 72, C), bf16),
        in_specs=[VMEM],
        out_specs=VMEM,
        scratch_shapes=[pltpu.VMEM((1024, 2304), bf16), pltpu.VMEM((192, C), f32), pltpu.VMEM((2304, C), f32)],
        compiler_params=PARAMS,
        cost_estimate=pl.CostEstimate(flops=2 * 1024 * 2304 * 256, bytes_accessed=8 * 1024 * 1024, transcendentals=0),
        name="kernel_grads",
    )(acts)


def turn(value, axis, by):
    size = lax.axis_size(axis)
    return lax.ppermute(value, axis, [(i, (i + by) % size) for i in range(size)])


def apart(value, by):
    pairs = [(2 * i + c, 2 * (i + d) + c) for c, d in ((0, by), (1, -by)) for i in range(8) if 0 <= i + d < 8]
    return lax.ppermute(value, ("z", "core"), pairs)


def around(value, by):
    return lax.ppermute(value, ("y", "core"), [(i, (i + by) % 8) for i in range(8)])


def unpack_kernel(*refs):
    place = 2 * lax.axis_index("y") + lax.axis_index("core")
    for d in range(8):
        at = pl.multiple_of(lax.rem(place + 8 - d, 8) * 16, 16)
        refs[8][pl.ds(at, 16), :] = refs[d][:, 0:2 * C]
        refs[9][pl.ds(at, 16), :] = refs[d][:, 2 * C:4 * C]


def unpack(back):
    return pl.pallas_call(
        unpack_kernel,
        out_shape=[jax.ShapeDtypeStruct((128, 2 * C), bf16)] * 2,
        in_specs=[VMEM] * 8,
        out_specs=[VMEM] * 2,
        compiler_params=PARAMS,
        name="unpack",
    )(*back)


def local(block_out, out_grad, weights):
    core = lax.axis_index("core")

    pieces, part = make_pieces(block_out[0, 0], out_grad[0, 0], weights[0])
    part = turn(part, "section", 2)
    beside = [lax.ppermute(weights[0, i], ("core", "section"),
                           [(4 * c + i, 4 * c + (i + (-1, 1)[c]) % 4) for c in range(2) for i in range(4)])
              for i in range(2)]

    tile = lax.all_to_all(pieces, ("y", "core"), 0, 0)
    part = repeat(part)
    tile, part = lax.optimization_barrier((tile, part))
    beyond = apart(tile, 1)
    far = apart(jnp.where(core == 0, tile[7, :WIDE + 16], tile[0, :WIDE + 16]), 2)
    quarters = lax.all_to_all(part, "y", 0, 0)

    beyond, far, beside, quarters = lax.optimization_barrier((beyond, far, beside, quarters))
    moved = [v for m in (*beside, quarters) for v in (m, turn(m, "core", 1))]
    fields = (tile, beyond, turn(beyond, "core", 1), far, turn(far, "core", 1))
    done, acts = blocks(fields, (weights[0], *moved))

    back = [done[0]] + [around(done[d], d) for d in range(1, 8)]
    got = lax.all_to_all(acts, ("core", "section"), 0, 0)
    got, back = lax.optimization_barrier((got, back))
    grad = kernel_grads(got)
    restored, input_grad = unpack(back)
    terms = [grad[0]] + [turn(grad[d], "y", d) for d in (1, 2, 3)]
    grad = sum(t.astype(f32) for t in terms).astype(bf16)
    grad = lax.all_to_all(grad, "z", 0, 0).astype(f32).sum(axis=0)
    here = lax.dynamic_slice_in_dim(grad, 36 * core, 36, 0)
    there = turn(lax.dynamic_slice_in_dim(grad, 36 * (1 - core), 36, 0), "core", 1)
    grad = jnp.where(core == 0, jnp.stack([here, there]), jnp.stack([there, here]))
    return restored[None, None], input_grad[None, None], (grad * (1.0 / math.sqrt(32768)))[None]


def solution(mesh):
    fine = Mesh(mesh.devices.reshape(8, 4, 2, 4), ("z", "y", "core", "section"))
    rows = ("z", "y", "core")
    spec = P("section", rows, None, None)
    return jax.shard_map(
        local,
        mesh=fine,
        in_specs=(spec, spec, P("section", None, None, None)),
        out_specs=(spec, spec, P("section", None, rows, None)),
        check_vma=False,
    )
```
